512 devices in a mesh: sx: 32 (over z, core), sy: 16 (over y, x).
Axes of the slice: x: 4, y: 4, z: 16, core: 2. Of those that a mesh axis runs over, the one named last changes fastest.
Arguments:
- local_source: float32 [32, 16, 768, 256], P('sx', 'sy'), may hold values from -6 to 6
- schur: bfloat16 [32, 16, 768, 768], P('sx', 'sy')
- local_inverse: bfloat16 [32, 16, 768, 768], P('sx', 'sy')
- primal_basis: bfloat16 [32, 16, 768, 32], P('sx', 'sy'), may hold values from -0.21875 to 0.21875
- coarse_inverse: float32 [32, 16, 32, 32], P('sx', 'sy')
- primal_map: int32 [32, 16, 32], P('sx', 'sy'), may hold values from 0 to 1023, as said below
- shared_count: int32 [32, 16, 8], P('sx', 'sy'), may hold values from 0 to 64, as said below
- row_order: int32 [32, 16, 768], P('sx', 'sy'), may hold values from 0 to 767, each once within a row
Outputs:
- solution: float32 [32, 16, 768, 256], P('sx', 'sy')
- residual: float32 [32, 16, 768, 256], P('sx', 'sy')
The draws below stay inside these ranges and needn't reach their ends.
Inputs may be any that keep to these rules, and one draw needn't show every extreme that they name: shared_count[i, j, d] equals shared_count[i + a, j + b, 7 - d] for offset d = (a, b), and is 0 where (i + a, j + b) lies outside the 32 x 16 grid. A neighbour at offset (0, 1), (0, -1), (1, 0) or (-1, 0) inside the grid shares a quarter of 64 rows or more; a diagonal neighbour shares none or a quarter of 64 or more. Some pair shares exactly 64. primal_map[i, j, m] lies in block (i - 1) mod 32, i or (i + 1) mod 32, block b holding the coarse unknowns b * 32 to (b + 1) * 32 - 1. Each subdomain's row_order holds every row once.
All inputs are finite; a program needn't handle non-finite values.
Results may differ from the reference program's by a relative error of at most 0.0072.
Values sent between devices are 32-bit elements; how exact they have to be, the bound alone decides.
No kernel may reach another device: no remote copies, remote signals or barrier semaphores. Data moves between devices by JAX's collectives and lax.ppermute only.
A program may use at most 64 MiB of HBM per device.

```python
import math
from functools import partial
import jax
import jax.numpy as jnp
from jax import lax

NI = 768
NPRIM = 32
CB = 32
MROW = 64
P_SIZE = 256
ITERS = 3
N_SX = 32
N_SY = 16


directions = ((-1, -1), (-1, 0), (-1, 1), (0, -1), (0, 1), (1, -1), (1, 0), (1, 1))


def symmetric_noise(key, order, strength):
    raw = jax.random.normal(key, (order, order), jnp.float32)
    return (raw + raw.T) * (strength / math.sqrt(2.0 * order))


def subdomain_pair(key):
    first_key, second_key, third_key = jax.random.split(key, 3)
    scales = jnp.exp(jax.random.uniform(first_key, (NI,), jnp.float32, math.log(0.5), math.log(2.0)))
    coupling = symmetric_noise(second_key, NI, 0.35)
    extra = symmetric_noise(third_key, NI, 0.12)
    root = jnp.sqrt(scales)
    identity = jnp.eye(NI, dtype=jnp.float32)
    schur_block = root[:, None] * (identity + coupling) * root[None, :]
    inverse_block = (identity - coupling + extra) / (root[:, None] * root[None, :])
    return (schur_block, inverse_block)


def draw_schur(key, part):
    keys = jax.random.split(jax.random.fold_in(key, 11), N_SX * N_SY)
    blocks = lax.map(lambda one: subdomain_pair(one)[0], keys)
    return blocks.reshape(N_SX, N_SY, NI, NI).astype(jnp.bfloat16)


def draw_local_inverse(key, part):
    keys = jax.random.split(jax.random.fold_in(key, 11), N_SX * N_SY)
    blocks = lax.map(lambda one: subdomain_pair(one)[1], keys)
    return blocks.reshape(N_SX, N_SY, NI, NI).astype(jnp.bfloat16)


def coarse_block(key):
    first_key, second_key = jax.random.split(key)
    scales = jnp.exp(jax.random.uniform(first_key, (CB,), jnp.float32, math.log(0.5), math.log(2.0)))
    root = jnp.sqrt(scales)
    noise = symmetric_noise(second_key, CB, 0.3)
    return root[:, None] * (jnp.eye(CB, dtype=jnp.float32) + noise) * root[None, :]


def draw_coarse_inverse(key, part):
    keys = jax.random.split(jax.random.fold_in(key, 23), N_SX * N_SY)
    blocks = lax.map(coarse_block, keys)
    return blocks.reshape(N_SX, N_SY, CB, CB).astype(jnp.float32)


def draw_primal_map(key, part):
    first_key, second_key = jax.random.split(jax.random.fold_in(key, 31))
    offset = jax.random.randint(first_key, (N_SX, N_SY, NPRIM), -1, 2)
    within = jax.random.randint(second_key, (N_SX, N_SY, NPRIM), 0, CB)
    first_index = jnp.arange(N_SX, dtype=jnp.int32)[:, None, None]
    block = (first_index + offset + N_SX) % N_SX
    return (block * CB + within).astype(jnp.int32)


def shifted(values, first, second):
    padded = jnp.pad(values, ((1, 1), (1, 1)))
    return padded[1 + first:1 + first + N_SX, 1 + second:1 + second + N_SY]


def draw_shared_count(key, part):
    first_key, second_key, third_key, fourth_key = jax.random.split(jax.random.fold_in(key, 41), 4)
    forward = jax.random.randint(first_key, (N_SX, N_SY, 4), MROW // 4, MROW + 1)
    present = jax.random.randint(second_key, (N_SX, N_SY, 4), 0, 2)
    diagonal = jnp.array([0, 1, 0, 1], dtype=jnp.int32)
    forward = forward * (1 - diagonal + diagonal * present)
    chosen_row = jax.random.randint(third_key, (), 0, N_SX - 1)
    chosen_col = jax.random.randint(fourth_key, (), 0, N_SY)
    row_index = jnp.arange(N_SX, dtype=jnp.int32)[:, None]
    col_index = jnp.arange(N_SY, dtype=jnp.int32)[None, :]
    hit = (row_index == chosen_row) & (col_index == chosen_col)
    forward = forward.at[:, :, 2].set(jnp.where(hit, MROW, forward[:, :, 2]))
    columns = []
    for place in range(4):
        first, second = directions[4 + place]
        inside = (row_index + first >= 0) & (row_index + first < N_SX) & (col_index + second >= 0) & (col_index + second < N_SY)
        columns.append(jnp.where(inside, forward[:, :, place], 0))
    counts = []
    for slot in range(8):
        if slot >= 4:
            counts.append(columns[slot - 4])
        else:
            first, second = directions[slot]
            counts.append(shifted(columns[7 - slot - 4], first, second))
    return jnp.stack(counts, axis=2).astype(jnp.int32)


def steps_of(rng, extent, cuts, low, largest):
    factor_of = 1.0
    for axis_at, blocks in cuts:
        draws = jax.random.uniform(jax.random.fold_in(jax.random.fold_in(rng, 6), axis_at), (blocks,), jnp.float32, low / len(cuts), largest / len(cuts))
        factor_of = factor_of * jnp.repeat(jnp.exp(draws), extent[axis_at] // blocks).reshape((-1,) + (1,) * (len(extent) - 1 - axis_at))
    return factor_of


def centred(rng, dims, scale, most, pieces=(), kind=jnp.bfloat16):
    gain = steps_of(rng, dims, pieces, -0.22, 0.18) if pieces else 1.0
    entries = jax.random.normal(rng, dims, jnp.float32) * scale * gain
    return jnp.minimum(jnp.maximum(entries, -most), most).astype(kind)


def setup_inputs(seed: int = 0) -> dict:
    key_of = jax.random.split(jax.random.key(seed), 9)
    return {
        "local_source": centred(key_of[0], (N_SX, N_SY, NI, P_SIZE), 1.0, 6.0, ((0, 32), (1, 16)), jnp.float32),
        "schur": draw_schur(jax.random.fold_in(key_of[8], 71), 0),
        "local_inverse": draw_local_inverse(jax.random.fold_in(key_of[8], 71), 0),
        "primal_basis": centred(key_of[3], (N_SX, N_SY, NI, NPRIM), NI ** -0.5, 0.21875, ((0, 32), (1, 16))),
        "coarse_inverse": draw_coarse_inverse(jax.random.fold_in(key_of[8], 71), 0),
        "primal_map": draw_primal_map(jax.random.fold_in(key_of[8], 71), 0),
        "shared_count": draw_shared_count(jax.random.fold_in(key_of[8], 71), 0),
        "row_order": jax.vmap(lambda own: jax.random.permutation(own, NI))(jax.random.split(key_of[7], N_SX * N_SY)).reshape((N_SX, N_SY, NI)).astype(jnp.int32),
    }


directions = ((-1, -1), (-1, 0), (-1, 1), (0, -1), (0, 1), (1, -1), (1, 0), (1, 1))
centre = 1.6
spread = 1.4


def group_rows(counts, order, rows):
    offsets = jnp.cumsum(counts) - counts
    column = jnp.arange(rows, dtype=jnp.int32)
    places = jnp.minimum(offsets[:, None] + column[None, :], order.shape[0] - 1).astype(jnp.int32)
    row_map = order[places]
    valid = (column[None, :] < counts[:, None]).astype(jnp.float32)
    return row_map, valid


def neighbour(values, first, second):
    widths = ((1, 1), (1, 1)) + ((0, 0),) * (values.ndim - 2)
    padded = jnp.pad(values, widths)
    return padded[1 + first:1 + first + N_SX, 1 + second:1 + second + N_SY]


def deposit(vector, row_map, incoming):
    return vector.at[row_map.reshape(-1)].add(incoming.reshape(-1, vector.shape[-1]))


def assemble(vector, row_map, valid):
    index = row_map.reshape(N_SX, N_SY, 8 * MROW, 1)
    taken = jnp.take_along_axis(vector, index, axis=2).reshape(N_SX, N_SY, 8, MROW, P_SIZE)
    taken = taken * valid[..., None]
    incoming = jnp.stack([neighbour(taken[:, :, 7 - slot], directions[slot][0], directions[slot][1]) for slot in range(8)], axis=2)
    incoming = incoming * valid[..., None]
    return jax.vmap(jax.vmap(deposit))(vector, row_map, incoming)


def batched(left, right):
    flat_left = left.reshape((-1,) + left.shape[2:])
    flat_right = right.reshape((-1,) + right.shape[2:])
    out = lax.map(lambda pair: jnp.dot(pair[0], pair[1], preferred_element_type=jnp.float32), (flat_left, flat_right))
    return out.reshape(left.shape[:2] + out.shape[1:])


def batched_left_t(left, right):
    flat_left = left.reshape((-1,) + left.shape[2:])
    flat_right = right.reshape((-1,) + right.shape[2:])
    out = lax.map(lambda pair: lax.dot_general(pair[0], pair[1], (((0,), (0,)), ((), ())), preferred_element_type=jnp.float32), (flat_left, flat_right))
    return out.reshape(left.shape[:2] + out.shape[1:])


def reference(local_source, schur, local_inverse, primal_basis, coarse_inverse, primal_map, shared_count, row_order):
    row_map, valid = jax.vmap(jax.vmap(partial(group_rows, rows=MROW)))(shared_count, row_order)
    marks = jax.vmap(jax.vmap(lambda rm, va: jnp.zeros((NI,), jnp.float32).at[rm.reshape(-1)].add(va.reshape(-1))))(row_map, valid)
    weight = (1.0 - 0.5 * marks)[..., None]
    column_ids = jnp.broadcast_to(jnp.arange(N_SY, dtype=jnp.int32)[None, :, None], primal_map.shape)

    def precondition(residual):
        scaled = (weight * residual).astype(jnp.bfloat16)
        local = batched(local_inverse, scaled)
        primal = batched_left_t(primal_basis, scaled)
        coarse_rhs = jnp.zeros((N_SY, N_SX * CB, P_SIZE), jnp.float32).at[column_ids, primal_map].add(primal)
        blocks = coarse_rhs.reshape(N_SY, N_SX, CB, P_SIZE)
        solved = jnp.einsum('ijab,jibp->ijap', coarse_inverse, blocks, precision=lax.Precision.HIGHEST)
        column_sol = jnp.transpose(solved, (1, 0, 2, 3)).reshape(N_SY, N_SX * CB, P_SIZE)
        picked = column_sol[column_ids, primal_map].astype(jnp.bfloat16)
        local = local + batched(primal_basis, picked)
        return assemble(weight * local, row_map, valid)

    right = assemble(local_source, row_map, valid)
    solution = jnp.zeros_like(right)
    residual = right
    sigma = centre / spread
    rho = 1.0 / sigma
    direction = jnp.zeros_like(right)
    for step in range(ITERS):
        update = precondition(residual)
        if step == 0:
            direction = update / centre
            rho = 1.0 / sigma
        else:
            rho_new = 1.0 / (2.0 * sigma - rho)
            direction = (rho_new * rho) * direction + (2.0 * rho_new / spread) * update
            rho = rho_new
        solution = solution + direction
        image = assemble(batched(schur, direction.astype(jnp.bfloat16)), row_map, valid)
        residual = residual - image
    return solution, residual
```

```python
from functools import partial

import jax
import jax.numpy as jnp
from jax import lax
from jax.experimental import pallas as pl
from jax.experimental.pallas import tpu as pltpu
from jax.sharding import PartitionSpec as P

MROW = 64
TILE = 8
ITERS = 3
centre = 1.6
spread = 1.4

SIDES = ((1, 1), (1, 0), (1, -1), (-1, 1), (-1, 0), (-1, -1), (0, 1), (0, -1))

VMEM = pl.BlockSpec(memory_space=pltpu.VMEM)
SMEM = pl.BlockSpec(memory_space=pltpu.SMEM)
F32 = jnp.float32
BF16 = jnp.bfloat16
HIGH = lax.Precision.HIGHEST


def swap(x, axis, side, wrap=False):
    n = lax.axis_size(axis)
    if side == 0:
        pairs = [(i, i ^ 1) for i in range(n)]
    else:
        pairs = [(i, ((i + 1) ^ 1) - 1) for i in range(n)]
        if wrap:
            pairs = [(i, p % n) for i, p in pairs]
        else:
            pairs = [(i, p) for i, p in pairs if 0 <= p < n]
    return lax.ppermute(x, axis, pairs)


def groups_of(ids, counts):
    alpha = 1 - 2 * lax.rem(ids[0], 2)
    gamma = 1 - 2 * lax.rem(ids[1], 2)
    size = [counts[d] for d in range(8)]
    out = []
    for s, t in SIDES:
        raw = 3 * (s * alpha + 1) + (t * gamma + 1)
        d = jnp.where(raw > 4, raw - 1, raw)
        start = jnp.int32(0)
        for e in range(8):
            start = start + jnp.where(e < d, size[e], 0)
        out.append((start, counts[d]))
    total = size[0]
    for e in range(1, 8):
        total = total + size[e]
    return out, total


def to_sorted(order):
    n = order.shape[1]
    column = jnp.transpose(jnp.broadcast_to(order, (128, n)))[:, :1]
    return (lax.broadcasted_iota(jnp.int32, (n, n), 1) == column).astype(F32).astype(BF16)


def from_sorted(order):
    n = order.shape[1]
    return (lax.broadcasted_iota(jnp.int32, (n, n), 0) == order).astype(F32).astype(BF16)


def moved(onehot, x):
    high = x.astype(BF16)
    rest = x - high.astype(F32)
    mid = rest.astype(BF16)
    low = (rest - mid.astype(F32)).astype(BF16)
    dot = partial(jnp.dot, onehot, preferred_element_type=F32)
    return dot(high) + dot(mid) + dot(low)


def window(start):
    skip = lax.rem(start, TILE)
    return pl.ds(pl.multiple_of(start - skip, TILE), MROW + TILE), skip


def emit(buf, groups, a_ref, b_ref, c_ref, d_ref):
    for k, (start, _) in enumerate(groups):
        place, skip = window(start)
        rows = pltpu.roll(buf[place, :], lax.rem(MROW + TILE - skip, MROW + TILE), 0)[0:MROW, :]
        if k < 3:
            a_ref[k * MROW:(k + 1) * MROW, :] = rows
        elif k < 6:
            b_ref[(k - 3) * MROW:(k - 2) * MROW, :] = rows
        elif k == 6:
            c_ref[...] = rows
        else:
            d_ref[...] = rows


def absorb(buf, groups, ra, rb, rc, rd):
    pieces = (rc[0:64, :], ra[64:128, :], rd[0:64, :], rc[128:192, :], rb[64:128, :], rd[128:192, :],
              rc[64:128, :], rd[64:128, :])
    at = lax.broadcasted_iota(jnp.int32, (MROW, 1), 0)
    tail = jnp.zeros((TILE, buf.shape[1]), F32)
    for (start, count), piece in zip(groups, pieces):
        place, skip = window(start)
        piece = jnp.concatenate([jnp.where(at < count, piece, 0.0), tail], axis=0)
        buf[place, :] = buf[place, :] + pltpu.roll(piece, skip, 0)


def fill(buf, x):
    n = x.shape[0]
    buf[0:n, :] = x
    buf[n:n + MROW + TILE, :] = jnp.zeros((MROW + TILE, x.shape[1]), F32)


def weights(n, total):
    return jnp.where(lax.broadcasted_iota(jnp.int32, (n, 1), 0) < total, 0.5, 1.0).astype(F32)


def chooser(ids, blocks, peers, size):
    alpha = 1 - 2 * lax.rem(ids[0], 2)
    n = blocks.shape[1]
    rows = lax.broadcasted_iota(jnp.int32, (size, n), 0)
    parts = []
    for shift in (0, 1, -1):
        want = lax.rem(ids[0] + shift * alpha + peers, peers) * size
        parts.append((blocks - want == rows).astype(F32))
    return jnp.concatenate(parts, axis=0)


def k_first(ids, counts, order, source, inverse, sorted_ref, a_ref, b_ref, c_ref, d_ref, buf):
    groups, _ = groups_of(ids, counts)
    x = moved(to_sorted(order[...]), source[...])
    sorted_ref[...] = x
    fill(buf, x)
    emit(buf, groups, a_ref, b_ref, c_ref, d_ref)
    n = inverse.shape[0]
    b_ref[3 * MROW:3 * MROW + n, :] = jnp.zeros((n, b_ref.shape[1]), F32)
    b_ref[3 * MROW:3 * MROW + n, 0:n] = inverse[...]


def k_sort(order, local, schur, basis, local_ref, schur_ref, basis_ref, onehot):
    onehot[...] = to_sorted(order[...])
    n = local.shape[0]
    step = 256
    dot = partial(lax.dot_general, preferred_element_type=F32)
    basis_ref[...] = dot(onehot[...], basis[...], (((1,), (0,)), ((), ()))).astype(BF16)
    for at in range(0, n, step):
        rows = onehot[at:at + step, :]
        for src, dst in ((local, local_ref), (schur, schur_ref)):
            half = dot(rows, src[...], (((1,), (0,)), ((), ()))).astype(BF16)
            dst[at:at + step, :] = dot(half, onehot[...], (((1,), (1,)), ((), ()))).astype(BF16)


def k_residual(first, peers, size, ids, counts, blocks, basis, old, product, ra, rb, rc, rd,
               res_ref, scaled_ref, give_ref, keep_ref, buf):
    groups, total = groups_of(ids, counts)
    if first:
        fill(buf, old[...])
    else:
        fill(buf, product[...])
    absorb(buf, groups, ra, rb, rc, rd)
    n = old.shape[0]
    res = buf[0:n, :] if first else old[...] - buf[0:n, :]
    res_ref[...] = res
    scaled = (weights(n, total) * res).astype(BF16)
    scaled_ref[...] = scaled
    primal = lax.dot_general(basis[...], scaled, (((0,), (0,)), ((), ())), preferred_element_type=F32)
    select = chooser(ids, blocks[...], peers, size)
    spread_out = jnp.dot(select, primal, precision=HIGH, preferred_element_type=F32)
    give_ref[...] = spread_out[size:2 * size, :]
    keep_ref[0:size, :] = spread_out[0:size, :]
    keep_ref[size:2 * size, :] = spread_out[2 * size:3 * size, :]


def k_local(local, scaled, out):
    out[...] = jnp.dot(local[...], scaled[...], preferred_element_type=F32)


def k_coarse(size, inv, inv_b, mine, theirs, own_ref, b_ref):
    dot = partial(jnp.dot, precision=HIGH, preferred_element_type=F32)
    own_ref[...] = dot(inv[...], mine[0:size, :] + theirs[size:2 * size, :])
    b_ref[...] = dot(inv_b[:, 0:size], theirs[0:size, :] + mine[size:2 * size, :])


def k_update(peers, size, ids, counts, blocks, basis, local, sol, sol_a, sol_b,
             up_ref, a_ref, b_ref, c_ref, d_ref, buf):
    groups, total = groups_of(ids, counts)
    select = chooser(ids, blocks[...], peers, size)
    stack = jnp.concatenate([sol[...], sol_a[...], sol_b[...]], axis=0)
    picked = lax.dot_general(select, stack, (((0,), (0,)), ((), ())), precision=HIGH, preferred_element_type=F32)
    n = local.shape[0]
    up = local[...] + jnp.dot(basis[...], picked.astype(BF16), preferred_element_type=F32)
    up = weights(n, total) * up
    up_ref[...] = up
    fill(buf, up)
    emit(buf, groups, a_ref, b_ref, c_ref, d_ref)


def k_apply(keep, gain, ids, counts, schur, up, old, ra, rb, rc, rd, dir_ref, v_ref, a_ref, b_ref, c_ref, d_ref, buf):
    groups, _ = groups_of(ids, counts)
    fill(buf, up[...])
    absorb(buf, groups, ra, rb, rc, rd)
    n = up.shape[0]
    direction = gain * buf[0:n, :]
    if keep is not None:
        direction = keep * old[...] + direction
    dir_ref[...] = direction
    v = jnp.dot(schur[...], direction.astype(BF16), preferred_element_type=F32)
    v_ref[...] = v
    buf[0:n, :] = v
    emit(buf, groups, a_ref, b_ref, c_ref, d_ref)


def k_solution(order, one, two, three, out):
    out[...] = moved(from_sorted(order[...]), one[...] + two[...] + three[...])


def k_final(ids, counts, order, old, product, ra, rb, rc, rd, out, buf):
    groups, _ = groups_of(ids, counts)
    fill(buf, product[...])
    absorb(buf, groups, ra, rb, rc, rd)
    n = old.shape[0]
    out[...] = moved(from_sorted(order[...]), old[...] - buf[0:n, :])


def call(kernel, ins, outs, flops, scratch=(), scalars=0):
    moved_bytes = sum(x.size * x.dtype.itemsize for x in ins)
    moved_bytes += sum(x.size * x.dtype.itemsize for x in outs)
    return pl.pallas_call(
        kernel,
        out_shape=tuple(outs),
        in_specs=[SMEM] * scalars + [VMEM] * (len(ins) - scalars),
        out_specs=tuple([VMEM] * len(outs)),
        scratch_shapes=list(scratch),
        compiler_params=pltpu.CompilerParams(vmem_limit_bytes=28 * 1024 * 1024),
        cost_estimate=pl.CostEstimate(flops=flops, bytes_accessed=moved_bytes, transcendentals=0),
    )(*ins)


def exchange(a, b, c, d, wrap=False):
    rb = swap(b, "sx", 1, wrap)
    ra = swap(a, "sx", 0)
    to_d = jnp.concatenate([ra[128:192], d, rb[128:192]], axis=0)
    to_c = jnp.concatenate([ra[0:64], c, rb[0:64]], axis=0)
    rd = swap(to_d, "sy", 1)
    rc = swap(to_c, "sy", 0)
    return ra, rb, rc, rd


def body(local_source, schur, local_inverse, primal_basis, coarse_inverse, primal_map, shared_count, row_order):
    source = local_source[0, 0]
    n, cols = source.shape
    inv = coarse_inverse[0, 0]
    size = inv.shape[0]
    modes = primal_basis.shape[3]
    peers = lax.axis_size("sx")
    ids = jnp.stack([lax.axis_index("sx"), lax.axis_index("sy")]).astype(jnp.int32)
    counts = shared_count[0, 0]
    order = row_order[0]
    blocks = primal_map[0]

    f32 = lambda *shape: jax.ShapeDtypeStruct(shape, F32)
    b16 = lambda *shape: jax.ShapeDtypeStruct(shape, BF16)
    full = f32(n, cols)
    sent = [f32(3 * MROW, cols), f32(3 * MROW, cols), f32(MROW, cols), f32(MROW, cols)]
    buf = [pltpu.VMEM((n + MROW + TILE, cols), F32)]
    big = 2 * n * n * cols

    src, *out = call(
        k_first,
        (ids, counts, order, source, inv),
        [full, sent[0], f32(3 * MROW + size, cols), sent[2], sent[3]],
        3 * big, buf, 2,
    )
    a_s, s_s, basis = call(
        k_sort,
        (order, local_inverse[0, 0], schur[0, 0], primal_basis[0, 0]),
        [b16(n, n), b16(n, n), b16(n, modes)],
        8 * n * n * n, [pltpu.VMEM((n, n), BF16)],
    )
    got = exchange(*out, wrap=True)
    inv_b = got[1][3 * MROW:3 * MROW + size]

    res, product, direction = src, src, src
    directions = []
    sigma = centre / spread
    rho = 1.0 / sigma
    for step in range(ITERS):
        res, scaled, give, kept = call(
            partial(k_residual, step == 0, peers, size),
            (ids, counts, blocks, basis, res, product, *got),
            [full, b16(n, cols), f32(size, cols), f32(2 * size, cols)],
            2 * n * modes * cols, buf, 2,
        )
        from_a = swap(give, "sx", 0)
        mine = jnp.concatenate([kept[0:size] + from_a, kept[size:2 * size]], axis=0)
        theirs = swap(mine, "sx", 1, True)
        local, = call(k_local, (a_s, scaled), [full], big)
        sol, sol_b = call(
            partial(k_coarse, size), (inv, inv_b, mine, theirs), [f32(size, cols), f32(size, cols)],
            4 * size * size * cols,
        )
        sol_a = swap(sol, "sx", 0)
        up, *out = call(
            partial(k_update, peers, size),
            (ids, counts, blocks, basis, local, sol, sol_a, sol_b),
            [full] + sent, 2 * n * modes * cols, buf, 2,
        )
        got = exchange(*out)
        if step == 0:
            keep, gain = None, 1.0 / centre
        else:
            rho_new = 1.0 / (2.0 * sigma - rho)
            keep, gain = rho_new * rho, 2.0 * rho_new / spread
            rho = rho_new
        direction, product, *out = call(
            partial(k_apply, keep, gain),
            (ids, counts, s_s, up, direction, *got),
            [full, full] + sent, big, buf, 2,
        )
        directions.append(direction)
        got = exchange(*out)
    total, = call(k_solution, (order, *directions), [full], 3 * big)
    residual, = call(k_final, (ids, counts, order, res, product, *got), [full], 3 * big, buf, 2)
    return total[None, None], residual[None, None]


def solution(mesh):
    four = P("sx", "sy", None, None)
    three = P("sx", "sy", None)
    return jax.shard_map(
        body,
        mesh=mesh,
        in_specs=(four, four, four, four, four, three, three, three),
        out_specs=(four, four),
        check_vma=False,
    )
```

```python
from functools import partial

import jax
import jax.numpy as jnp
from jax import lax
from jax.experimental import pallas as pl
from jax.experimental.pallas import tpu as pltpu
from jax.sharding import PartitionSpec as P

MROW = 64
TILE = 8
ITERS = 3
centre = 1.6
spread = 1.4

SIDES = ((1, 1), (1, 0), (1, -1), (-1, 1), (-1, 0), (-1, -1), (0, 1), (0, -1))

VMEM = pl.BlockSpec(memory_space=pltpu.VMEM)
SMEM = pl.BlockSpec(memory_space=pltpu.SMEM)
F32 = jnp.float32
BF16 = jnp.bfloat16
HIGH = lax.Precision.HIGHEST


def swap(x, axis, side, wrap=False):
    n = lax.axis_size(axis)
    if side == 0:
        pairs = [(i, i ^ 1) for i in range(n)]
    else:
        pairs = [(i, ((i + 1) ^ 1) - 1) for i in range(n)]
        if wrap:
            pairs = [(i, p % n) for i, p in pairs]
        else:
            pairs = [(i, p) for i, p in pairs if 0 <= p < n]
    return lax.ppermute(x, axis, pairs)


def pair(x, axis, side):
    n = lax.axis_size(axis)
    if side == 0:
        pairs = [[i, i + 1] for i in range(0, n, 2)]
    else:
        pairs = [[i, (i + 1) % n] for i in range(1, n, 2)]
    return lax.all_gather(x, axis, axis_index_groups=pairs, tiled=True)


def partner_half(side, axis):
    odd = lax.rem(lax.axis_index(axis), 2)
    return 1 - odd if side == 0 else odd


def half_of(ref, axis, side, rows, at=0, take=None):
    take = rows if take is None else take
    if ref.shape[0] != 2 * rows:
        return ref[at:at + take, :]
    return ref[pl.ds(pl.multiple_of(partner_half(side, axis) * rows, TILE) + at, take), :]


def here():
    return lax.axis_index("sx"), lax.axis_index("sy")


def table_of(counts):
    i, j = here()
    alpha = 1 - 2 * lax.rem(i, 2)
    gamma = 1 - 2 * lax.rem(j, 2)
    size = [counts[d] for d in range(8)]
    first = [jnp.int32(0)]
    for d in range(8):
        first.append(first[d] + size[d])
    starts, sizes = [], []
    for s, t in SIDES:
        raw = 3 * (s * alpha + 1) + (t * gamma + 1)
        d = jnp.where(raw > 4, raw - 1, raw)
        start, count = first[0], size[0]
        for e in range(1, 8):
            start = jnp.where(d == e, first[e], start)
            count = jnp.where(d == e, size[e], count)
        starts.append(start)
        sizes.append(count)
    return starts, sizes, first[8]


def groups_of(table):
    return [(table[0, k], table[0, 8 + k]) for k in range(8)]


def to_sorted(order):
    n = order.shape[1]
    column = jnp.transpose(jnp.broadcast_to(order, (128, n)))[:, :1]
    return (lax.broadcasted_iota(jnp.int32, (n, n), 1) == column).astype(F32).astype(BF16)


def from_sorted(order):
    n = order.shape[1]
    return (lax.broadcasted_iota(jnp.int32, (n, n), 0) == order).astype(F32).astype(BF16)


def moved(onehot, x):
    high = x.astype(BF16)
    rest = x - high.astype(F32)
    mid = rest.astype(BF16)
    low = (rest - mid.astype(F32)).astype(BF16)
    dot = partial(jnp.dot, onehot, preferred_element_type=F32)
    return dot(high) + dot(mid) + dot(low)


def window(start):
    skip = lax.rem(start, TILE)
    return pl.ds(pl.multiple_of(start - skip, TILE), MROW + TILE), skip


def emit(buf, groups, a_ref, b_ref, c_ref, d_ref):
    for k, (start, _) in enumerate(groups):
        place, skip = window(start)
        rows = pltpu.roll(buf[place, :], lax.rem(MROW + TILE - skip, MROW + TILE), 0)[0:MROW, :]
        if k < 3:
            a_ref[k * MROW:(k + 1) * MROW, :] = rows
        elif k < 6:
            b_ref[(k - 3) * MROW:(k - 2) * MROW, :] = rows
        elif k == 6:
            c_ref[...] = rows
        else:
            d_ref[...] = rows


def absorb(buf, groups, ra, rb, rc, rd):
    edge_a = half_of(ra, "sx", 0, 3 * MROW, MROW, MROW)
    pieces = [half_of(rc, "sy", 0, 3 * MROW, k * MROW, MROW) for k in range(3)]
    order = (pieces[0], edge_a, rd[0:64, :], pieces[2], rb[64:128, :], rd[128:192, :], pieces[1], rd[64:128, :])
    at = lax.broadcasted_iota(jnp.int32, (MROW, 1), 0)
    tail = jnp.zeros((TILE, buf.shape[1]), F32)
    for (start, count), piece in zip(groups, order):
        place, skip = window(start)
        piece = jnp.concatenate([jnp.where(at < count, piece, 0.0), tail], axis=0)
        buf[place, :] = buf[place, :] + pltpu.roll(piece, skip, 0)


def fill(buf, x):
    n = x.shape[0]
    buf[0:n, :] = x
    buf[n:n + MROW + TILE, :] = jnp.zeros((MROW + TILE, x.shape[1]), F32)


def weights(n, table):
    total = jnp.max(table[1:2, :], axis=1, keepdims=True)
    return jnp.where(lax.broadcasted_iota(jnp.int32, (n, 1), 0) < total, 0.5, 1.0).astype(F32)


def chooser(blocks, peers, size):
    mine = lax.axis_index("sx")
    alpha = 1 - 2 * lax.rem(mine, 2)
    n = blocks.shape[1]
    rows = lax.broadcasted_iota(jnp.int32, (size, n), 0)
    parts = []
    for shift in (0, 1, -1):
        want = lax.rem(mine + shift * alpha + peers, peers) * size
        parts.append((blocks - want == rows).astype(F32))
    return jnp.concatenate(parts, axis=0)


def k_first(counts, order, source, inverse, sorted_ref, table_ref, a_ref, b_ref, c_ref, d_ref, buf):
    starts, sizes, total = table_of(counts)
    at = lax.broadcasted_iota(jnp.int32, table_ref.shape, 1)
    row = lax.broadcasted_iota(jnp.int32, table_ref.shape, 0)
    table = jnp.full(table_ref.shape, total, jnp.int32)
    for k, value in enumerate(starts + sizes):
        table = jnp.where((row == 0) & (at == k), value, table)
    table_ref[...] = table
    x = moved(to_sorted(order[...]), source[...])
    sorted_ref[...] = x
    fill(buf, x)
    emit(buf, list(zip(starts, sizes)), a_ref, b_ref, c_ref, d_ref)
    n = inverse.shape[0]
    b_ref[3 * MROW:3 * MROW + n, :] = jnp.zeros((n, b_ref.shape[1]), F32)
    b_ref[3 * MROW:3 * MROW + n, 0:n] = inverse[...]


def k_relay(ra, rb, c, d, to_c, to_d):
    to_c[0:64, :] = half_of(ra, "sx", 0, 3 * MROW, 0, MROW)
    to_d[0:64, :] = half_of(ra, "sx", 0, 3 * MROW, 2 * MROW, MROW)
    to_c[64:128, :] = c[...]
    to_d[64:128, :] = d[...]
    to_c[128:192, :] = rb[0:64, :]
    to_d[128:192, :] = rb[128:192, :]


def k_sort(order, local, schur, basis, local_ref, schur_ref, basis_ref, onehot):
    onehot[...] = to_sorted(order[...])
    n = local.shape[0]
    step = 256
    dot = partial(lax.dot_general, preferred_element_type=F32)
    basis_ref[...] = dot(onehot[...], basis[...], (((1,), (0,)), ((), ()))).astype(BF16)
    for at in range(0, n, step):
        rows = onehot[at:at + step, :]
        for src, dst in ((local, local_ref), (schur, schur_ref)):
            half = dot(rows, src[...], (((1,), (0,)), ((), ()))).astype(BF16)
            dst[at:at + step, :] = dot(half, onehot[...], (((1,), (1,)), ((), ()))).astype(BF16)


def k_residual(first, peers, size, table, blocks, basis, old, product, ra, rb, rc, rd,
               res_ref, scaled_ref, give_ref, keep_ref, buf):
    groups = groups_of(table)
    if first:
        fill(buf, old[...])
    else:
        fill(buf, product[...])
    absorb(buf, groups, ra, rb, rc, rd)
    n = old.shape[0]
    res = buf[0:n, :] if first else old[...] - buf[0:n, :]
    res_ref[...] = res
    scaled = (weights(n, table) * res).astype(BF16)
    scaled_ref[...] = scaled
    primal = lax.dot_general(basis[...], scaled, (((0,), (0,)), ((), ())), preferred_element_type=F32)
    select = chooser(blocks[...], peers, size)
    spread_out = jnp.dot(select, primal, precision=HIGH, preferred_element_type=F32)
    give_ref[...] = spread_out[size:2 * size, :]
    keep_ref[0:size, :] = spread_out[0:size, :]
    keep_ref[size:2 * size, :] = spread_out[2 * size:3 * size, :]


def k_middle(size, kept, from_a, mine):
    mine[0:size, :] = kept[0:size, :] + half_of(from_a, "sx", 0, size)
    mine[size:2 * size, :] = kept[size:2 * size, :]


def k_coarse(size, inv, first_b, mine, theirs, own_ref, b_ref):
    dot = partial(jnp.dot, precision=HIGH, preferred_element_type=F32)
    their_own = half_of(theirs, "sx", 1, 2 * size, 0, size)
    their_mine = half_of(theirs, "sx", 1, 2 * size, size, size)
    inv_b = first_b[3 * MROW:3 * MROW + size, 0:size]
    own_ref[...] = dot(inv[...], mine[0:size, :] + their_mine)
    b_ref[...] = dot(inv_b, their_own + mine[size:2 * size, :])


def k_update(peers, size, table, blocks, basis, matrix, scaled, sol, sol_a, sol_b,
             up_ref, a_ref, b_ref, c_ref, d_ref, buf):
    groups = groups_of(table)
    select = chooser(blocks[...], peers, size)
    stack = jnp.concatenate([sol[...], half_of(sol_a, "sx", 0, size), sol_b[...]], axis=0)
    picked = lax.dot_general(select, stack, (((0,), (0,)), ((), ())), precision=HIGH, preferred_element_type=F32)
    n = scaled.shape[0]
    up = jnp.dot(matrix[...], scaled[...], preferred_element_type=F32)
    up = up + jnp.dot(basis[...], picked.astype(BF16), preferred_element_type=F32)
    up = weights(n, table) * up
    up_ref[...] = up
    fill(buf, up)
    emit(buf, groups, a_ref, b_ref, c_ref, d_ref)


def k_apply(keep, gain, table, schur, up, old, ra, rb, rc, rd, dir_ref, v_ref, a_ref, b_ref, c_ref, d_ref, buf):
    groups = groups_of(table)
    fill(buf, up[...])
    absorb(buf, groups, ra, rb, rc, rd)
    n = up.shape[0]
    direction = gain * buf[0:n, :]
    if keep is not None:
        direction = keep * old[...] + direction
    dir_ref[...] = direction
    v = jnp.dot(schur[...], direction.astype(BF16), preferred_element_type=F32)
    v_ref[...] = v
    buf[0:n, :] = v
    emit(buf, groups, a_ref, b_ref, c_ref, d_ref)


def k_solution(order, one, two, three, out):
    out[...] = moved(from_sorted(order[...]), one[...] + two[...] + three[...])


def k_final(table, order, old, product, ra, rb, rc, rd, out, buf):
    groups = groups_of(table)
    fill(buf, product[...])
    absorb(buf, groups, ra, rb, rc, rd)
    n = old.shape[0]
    out[...] = moved(from_sorted(order[...]), old[...] - buf[0:n, :])


def call(kernel, ins, outs, flops, scratch=(), scalars=0):
    moved_bytes = sum(x.size * x.dtype.itemsize for x in ins)
    moved_bytes += sum(x.size * x.dtype.itemsize for x in outs)
    return pl.pallas_call(
        kernel,
        out_shape=tuple(outs),
        in_specs=[SMEM] * scalars + [VMEM] * (len(ins) - scalars),
        out_specs=tuple([VMEM] * len(outs)),
        scratch_shapes=list(scratch),
        compiler_params=pltpu.CompilerParams(vmem_limit_bytes=28 * 1024 * 1024),
        cost_estimate=pl.CostEstimate(flops=flops, bytes_accessed=moved_bytes, transcendentals=0),
    )(*ins)


def exchange(a, b, c, d, hide=False):
    cols = c.shape[1]
    rb = swap(b, "sx", 1, b.shape[0] > 3 * MROW)
    ra = swap(a, "sx", 0) if hide else pair(a, "sx", 0)
    leg = jax.ShapeDtypeStruct((3 * MROW, cols), F32)
    to_c, to_d = call(k_relay, (ra, rb, c, d), [leg, leg], 0)
    rd = swap(to_d, "sy", 1)
    rc = swap(to_c, "sy", 0) if hide else pair(to_c, "sy", 0)
    return ra, rb, rc, rd


def body(local_source, schur, local_inverse, primal_basis, coarse_inverse, primal_map, shared_count, row_order):
    source = local_source[0, 0]
    n, cols = source.shape
    inv = coarse_inverse[0, 0]
    size = inv.shape[0]
    modes = primal_basis.shape[3]
    peers = lax.axis_size("sx")
    counts = shared_count[0, 0]
    order = row_order[0]
    blocks = primal_map[0]

    f32 = lambda *shape: jax.ShapeDtypeStruct(shape, F32)
    b16 = lambda *shape: jax.ShapeDtypeStruct(shape, BF16)
    full = f32(n, cols)
    sent = [f32(3 * MROW, cols), f32(3 * MROW, cols), f32(MROW, cols), f32(MROW, cols)]
    buf = [pltpu.VMEM((n + MROW + TILE, cols), F32)]
    big = 2 * n * n * cols

    src, table, *out = call(
        k_first,
        (counts, order, source, inv),
        [full, jax.ShapeDtypeStruct((8, 128), jnp.int32), sent[0], f32(3 * MROW + size, cols), sent[2], sent[3]],
        3 * big, buf, 1,
    )
    a_s, s_s, basis = call(
        k_sort,
        (order, local_inverse[0, 0], schur[0, 0], primal_basis[0, 0]),
        [b16(n, n), b16(n, n), b16(n, modes)],
        8 * n * n * n, [pltpu.VMEM((n, n), BF16)],
    )
    got = exchange(*out, hide=True)
    first_b = got[1]

    res, product, direction = src, src, src
    directions = []
    sigma = centre / spread
    rho = 1.0 / sigma
    for step in range(ITERS):
        res, scaled, give, kept = call(
            partial(k_residual, step == 0, peers, size),
            (table, blocks, basis, res, product, *got),
            [full, b16(n, cols), f32(size, cols), f32(2 * size, cols)],
            2 * n * modes * cols, buf,
        )
        from_a = pair(give, "sx", 0)
        mine, = call(partial(k_middle, size), (kept, from_a), [f32(2 * size, cols)], 0)
        theirs = pair(mine, "sx", 1)
        sol, sol_b = call(
            partial(k_coarse, size), (inv, first_b, mine, theirs), [f32(size, cols), f32(size, cols)],
            4 * size * size * cols,
        )
        sol_a = pair(sol, "sx", 0)
        up, *out = call(
            partial(k_update, peers, size),
            (table, blocks, basis, a_s, scaled, sol, sol_a, sol_b),
            [full] + sent, big, buf,
        )
        got = exchange(*out)
        if step == 0:
            keep, gain = None, 1.0 / centre
        else:
            rho_new = 1.0 / (2.0 * sigma - rho)
            keep, gain = rho_new * rho, 2.0 * rho_new / spread
            rho = rho_new
        direction, product, *out = call(
            partial(k_apply, keep, gain),
            (table, s_s, up, direction, *got),
            [full, full] + sent, big, buf,
        )
        directions.append(direction)
        got = exchange(*out, hide=step == ITERS - 1)
    total, = call(k_solution, (order, *directions), [full], 3 * big)
    residual, = call(k_final, (table, order, res, product, *got), [full], 3 * big, buf)
    return total[None, None], residual[None, None]


def solution(mesh):
    four = P("sx", "sy", None, None)
    three = P("sx", "sy", None)
    return jax.shard_map(
        body,
        mesh=mesh,
        in_specs=(four, four, four, four, four, three, three, three),
        out_specs=(four, four),
        check_vma=False,
    )
```

```python
from functools import partial

import jax
import jax.numpy as jnp
from jax import lax
from jax.experimental import pallas as pl
from jax.experimental.pallas import tpu as pltpu
from jax.sharding import PartitionSpec as P

MROW = 64
TILE = 8
ITERS = 3
centre = 1.6
spread = 1.4

SIDES = ((1, 1), (1, 0), (1, -1), (-1, 1), (-1, 0), (-1, -1), (0, 1), (0, -1))

VMEM = pl.BlockSpec(memory_space=pltpu.VMEM)
FAR = pl.BlockSpec(memory_space=pltpu.HBM)
LOOSE = pl.BlockSpec(memory_space=pl.ANY)
F32 = jnp.float32
BF16 = jnp.bfloat16
HIGH = lax.Precision.HIGHEST


def other(i, j, side):
    if side in "AB":
        return (i ^ 1 if side == "A" else ((i + 1) ^ 1) - 1), j
    return i, (j ^ 1 if (side == "C") == (i % 2 == 0) else ((j + 1) ^ 1) - 1)


def links(side):
    sizes = lax.axis_size("sx"), lax.axis_size("sy")
    for i in range(sizes[0]):
        for j in range(sizes[1]):
            yield sizes, (i, j), other(i, j, side)


def swap(x, side, wrap=False):
    pairs = []
    for (n, m), (i, j), (p, q) in links(side):
        if wrap or (0 <= p < n and 0 <= q < m):
            pairs.append((i * m + j, p % n * m + q % m))
    return lax.ppermute(x, ("sx", "sy"), pairs)


def leads(i, j, side):
    if side == "A":
        return 1 - i % 2
    if side == "B":
        return i % 2
    return (1 + i + j) % 2 if side == "C" else (i + j) % 2


def pair(x, side):
    pairs = []
    for (n, m), (i, j), (p, q) in links(side):
        if leads(i, j, side):
            pairs.append([i * m + j, p % n * m + q % m])
    return lax.all_gather(x, ("sx", "sy"), axis_index_groups=pairs, tiled=True)


def half_of(ref, side, rows, at=0, take=None):
    take = rows if take is None else take
    if ref.shape[0] != 2 * rows:
        return ref[at:at + take, :]
    return ref[pl.ds(pl.multiple_of(lax.rem(leads(*here(), side), 2) * rows, TILE) + at, take), :]


def here():
    return lax.axis_index("sx"), lax.axis_index("sy")


def table_of(counts):
    i, j = here()
    alpha = 1 - 2 * lax.rem(i, 2)
    gamma = 1 - 2 * lax.rem(i + j, 2)
    size = [counts[d] for d in range(8)]
    first = [jnp.int32(0)]
    for d in range(8):
        first.append(first[d] + size[d])
    starts, sizes = [], []
    for s, t in SIDES:
        raw = 3 * (s * alpha + 1) + (t * gamma + 1)
        d = jnp.where(raw > 4, raw - 1, raw)
        start, count = first[0], size[0]
        for e in range(1, 8):
            start = jnp.where(d == e, first[e], start)
            count = jnp.where(d == e, size[e], count)
        starts.append(start)
        sizes.append(count)
    return starts, sizes, first[8]


def groups_of(table):
    return [(table[0, k], table[0, 8 + k]) for k in range(8)]


def to_sorted(order):
    n = order.shape[1]
    column = jnp.transpose(jnp.broadcast_to(order, (128, n)))[:, :1]
    return (lax.broadcasted_iota(jnp.int32, (n, n), 1) == column).astype(F32).astype(BF16)


def from_sorted(order):
    n = order.shape[1]
    return (lax.broadcasted_iota(jnp.int32, (n, n), 0) == order).astype(F32).astype(BF16)


def moved(onehot, x):
    high = x.astype(BF16)
    rest = x - high.astype(F32)
    mid = rest.astype(BF16)
    low = (rest - mid.astype(F32)).astype(BF16)
    dot = partial(jnp.dot, onehot, preferred_element_type=F32)
    return dot(high) + dot(mid) + dot(low)


def window(start):
    skip = lax.rem(start, TILE)
    return pl.ds(pl.multiple_of(start - skip, TILE), MROW + TILE), skip


def emit(buf, groups, a_ref, b_ref, c_ref, d_ref):
    for k, (start, _) in enumerate(groups):
        place, skip = window(start)
        rows = pltpu.roll(buf[place, :], lax.rem(MROW + TILE - skip, MROW + TILE), 0)[0:MROW, :]
        if k < 3:
            a_ref[k * MROW:(k + 1) * MROW, :] = rows
        elif k < 6:
            b_ref[(k - 3) * MROW:(k - 2) * MROW, :] = rows
        elif k == 6:
            c_ref[...] = rows
        else:
            d_ref[...] = rows


def absorb(buf, groups, ra, rb, rc, rd):
    edge_a = half_of(ra, "A", 3 * MROW, MROW, MROW)
    pieces = [half_of(rc, "C", 3 * MROW, k * MROW, MROW) for k in range(3)]
    order = (pieces[0], edge_a, rd[0:64, :], pieces[2], rb[64:128, :], rd[128:192, :], pieces[1], rd[64:128, :])
    at = lax.broadcasted_iota(jnp.int32, (MROW, 1), 0)
    tail = jnp.zeros((TILE, buf.shape[1]), F32)
    for (start, count), piece in zip(groups, order):
        place, skip = window(start)
        piece = jnp.concatenate([jnp.where(at < count, piece, 0.0), tail], axis=0)
        buf[place, :] = buf[place, :] + pltpu.roll(piece, skip, 0)


def fill(buf, x):
    n = x.shape[0]
    buf[0:n, :] = x
    buf[n:n + MROW + TILE, :] = jnp.zeros((MROW + TILE, x.shape[1]), F32)


def weights(n, table):
    total = jnp.max(table[1:2, :], axis=1, keepdims=True)
    return jnp.where(lax.broadcasted_iota(jnp.int32, (n, 1), 0) < total, 0.5, 1.0).astype(F32)


def chooser(blocks, peers, size):
    mine = lax.axis_index("sx")
    alpha = 1 - 2 * lax.rem(mine, 2)
    n = blocks.shape[1]
    rows = lax.broadcasted_iota(jnp.int32, (size, n), 0)
    parts = []
    for shift in (0, 1, -1):
        want = lax.rem(mine + shift * alpha + peers, peers) * size
        parts.append((blocks - want == rows).astype(F32))
    return jnp.concatenate(parts, axis=0)


def k_first(counts_in, order_in, source_in, inverse_in, sorted_ref, table_ref, a_ref, b_ref, c_ref, d_ref,
            buf, counts, order, source, inverse, arrived):
    copies = [
        pltpu.make_async_copy(src, dst, arrived.at[k])
        for k, (src, dst) in enumerate(
            ((order_in, order), (counts_in, counts), (source_in, source), (inverse_in, inverse)))
    ]
    for copy in copies:
        copy.start()
    copies[0].wait()
    onehot = to_sorted(order[...])
    copies[1].wait()
    starts, sizes, total = table_of(counts)
    at = lax.broadcasted_iota(jnp.int32, table_ref.shape, 1)
    row = lax.broadcasted_iota(jnp.int32, table_ref.shape, 0)
    table = jnp.full(table_ref.shape, total, jnp.int32)
    for k, value in enumerate(starts + sizes):
        table = jnp.where((row == 0) & (at == k), value, table)
    table_ref[...] = table
    copies[2].wait()
    x = moved(onehot, source[...])
    sorted_ref[...] = x
    fill(buf, x)
    emit(buf, list(zip(starts, sizes)), a_ref, b_ref, c_ref, d_ref)
    n = inverse.shape[0]
    copies[3].wait()
    b_ref[3 * MROW:3 * MROW + n, :] = jnp.zeros((n, b_ref.shape[1]), F32)
    b_ref[3 * MROW:3 * MROW + n, 0:n] = inverse[...]


def k_relay(ra, rb, c, d, *rest):
    to_c, to_d = rest[-2:]
    to_c[0:64, :] = half_of(ra, "A", 3 * MROW, 2 * MROW, MROW)
    to_d[0:64, :] = half_of(ra, "A", 3 * MROW, 0, MROW)
    to_c[64:128, :] = c[...]
    to_d[64:128, :] = d[...]
    to_c[128:192, :] = rb[128:192, :]
    to_d[128:192, :] = rb[0:64, :]


def k_sort(order, matrix, *rest):
    onehot = rest[-1]
    onehot[...] = to_sorted(order[...])
    n = matrix.shape[0]
    step = 256
    dot = partial(lax.dot_general, preferred_element_type=F32)
    if len(rest) == 4:
        basis, out, basis_ref = rest[:3]
        basis_ref[...] = dot(onehot[...], basis[...], (((1,), (0,)), ((), ()))).astype(BF16)
    else:
        out = rest[0]
    for at in range(0, n, step):
        half = dot(onehot[at:at + step, :], matrix[...], (((1,), (0,)), ((), ()))).astype(BF16)
        out[at:at + step, :] = dot(half, onehot[...], (((1,), (1,)), ((), ()))).astype(BF16)


def k_residual(first, peers, size, table, blocks, basis, old, product, ra, rb, rc, rd,
               *rest):
    res_ref, scaled_ref, give_ref, keep_ref, buf = rest[-5:]
    groups = groups_of(table)
    if first:
        fill(buf, old[...])
    else:
        fill(buf, product[...])
    absorb(buf, groups, ra, rb, rc, rd)
    n = old.shape[0]
    res = buf[0:n, :] if first else old[...] - buf[0:n, :]
    res_ref[...] = res
    scaled = (weights(n, table) * res).astype(BF16)
    scaled_ref[...] = scaled
    primal = lax.dot_general(basis[...], scaled, (((0,), (0,)), ((), ())), preferred_element_type=F32)
    select = chooser(blocks[...], peers, size)
    spread_out = jnp.dot(select, primal, precision=HIGH, preferred_element_type=F32)
    give_ref[...] = spread_out[size:2 * size, :]
    keep_ref[0:size, :] = spread_out[0:size, :]
    keep_ref[size:2 * size, :] = spread_out[2 * size:3 * size, :]


def k_middle(size, kept, from_a, mine):
    mine[0:size, :] = kept[0:size, :] + half_of(from_a, "A", size)
    mine[size:2 * size, :] = kept[size:2 * size, :]


def k_coarse(size, inv, first_b, mine, theirs, own_ref, b_ref):
    dot = partial(jnp.dot, precision=HIGH, preferred_element_type=F32)
    their_own = half_of(theirs, "B", 2 * size, 0, size)
    their_mine = half_of(theirs, "B", 2 * size, size, size)
    inv_b = first_b[3 * MROW:3 * MROW + size, 0:size]
    own_ref[...] = dot(inv[...], mine[0:size, :] + their_mine)
    b_ref[...] = dot(inv_b, their_own + mine[size:2 * size, :])


def k_update(peers, size, table, blocks, basis, matrix, scaled, sol, sol_a, sol_b,
             up_ref, a_ref, b_ref, c_ref, d_ref, buf):
    groups = groups_of(table)
    select = chooser(blocks[...], peers, size)
    stack = jnp.concatenate([sol[...], half_of(sol_a, "A", size), sol_b[...]], axis=0)
    picked = lax.dot_general(select, stack, (((0,), (0,)), ((), ())), precision=HIGH, preferred_element_type=F32)
    n = scaled.shape[0]
    up = jnp.dot(matrix[...], scaled[...], preferred_element_type=F32)
    up = up + jnp.dot(basis[...], picked.astype(BF16), preferred_element_type=F32)
    up = weights(n, table) * up
    up_ref[...] = up
    fill(buf, up)
    emit(buf, groups, a_ref, b_ref, c_ref, d_ref)


def k_apply(keep, gain, table, schur, up, old, ra, rb, rc, rd, dir_ref, v_ref, a_ref, b_ref, c_ref, d_ref, buf):
    groups = groups_of(table)
    fill(buf, up[...])
    absorb(buf, groups, ra, rb, rc, rd)
    n = up.shape[0]
    direction = gain * buf[0:n, :]
    if keep is not None:
        direction = keep * old[...] + direction
    dir_ref[...] = direction
    v = jnp.dot(schur[...], direction.astype(BF16), preferred_element_type=F32)
    v_ref[...] = v
    buf[0:n, :] = v
    emit(buf, groups, a_ref, b_ref, c_ref, d_ref)


def k_solution(order, one, two, three, out, token):
    token[...] = jnp.zeros(token.shape, F32)
    out[...] = moved(from_sorted(order[...]), one[...] + two[...] + three[...])


def k_final(table, order, old, product, ra, rb, rc, rd, out, buf):
    groups = groups_of(table)
    fill(buf, product[...])
    absorb(buf, groups, ra, rb, rc, rd)
    n = old.shape[0]
    out[...] = moved(from_sorted(order[...]), old[...] - buf[0:n, :])


def call(kernel, ins, outs, flops, scratch=(), far=0, after=(), room=28):
    moved_bytes = sum(x.size * x.dtype.itemsize for x in ins)
    moved_bytes += sum(x.size * x.dtype.itemsize for x in outs)
    return pl.pallas_call(
        kernel,
        out_shape=tuple(outs),
        in_specs=[FAR] * far + [VMEM] * (len(ins) - far) + [LOOSE] * len(after),
        out_specs=tuple([VMEM] * len(outs)),
        scratch_shapes=list(scratch),
        compiler_params=pltpu.CompilerParams(vmem_limit_bytes=room * 1024 * 1024),
        cost_estimate=pl.CostEstimate(flops=flops, bytes_accessed=moved_bytes, transcendentals=0),
    )(*ins, *after)


def exchange(a, b, c, d, first=False, beside=()):
    leg = jax.ShapeDtypeStruct((3 * MROW, c.shape[1]), F32)
    rb = swap(b, "B", first)
    ra = swap(a, "A") if first else pair(a, "A")
    to_c, to_d = call(k_relay, (ra, rb, c, d), [leg, leg], 0, after=beside)
    rd = swap(to_d, "D")
    rc = swap(to_c, "C") if first else pair(to_c, "C")
    return ra, rb, rc, rd


def body(local_source, schur, local_inverse, primal_basis, coarse_inverse, primal_map, shared_count, row_order):
    source = local_source[0, 0]
    n, cols = source.shape
    inv = coarse_inverse[0, 0]
    size = inv.shape[0]
    modes = primal_basis.shape[3]
    peers = lax.axis_size("sx")
    counts = shared_count[0, 0]
    order = row_order[0]
    blocks = primal_map[0]

    f32 = lambda *shape: jax.ShapeDtypeStruct(shape, F32)
    b16 = lambda *shape: jax.ShapeDtypeStruct(shape, BF16)
    full = f32(n, cols)
    sent = [f32(3 * MROW, cols), f32(3 * MROW, cols), f32(MROW, cols), f32(MROW, cols)]
    buf = [pltpu.VMEM((n + MROW + TILE, cols), F32)]
    big = 2 * n * n * cols

    src, table, *out = call(
        k_first,
        (counts, order, source, inv),
        [full, jax.ShapeDtypeStruct((8, 128), jnp.int32), sent[0], f32(3 * MROW + size, cols), sent[2], sent[3]],
        2 * big,
        buf + [
            pltpu.SMEM((8,), jnp.int32), pltpu.VMEM(order.shape, jnp.int32), pltpu.VMEM((n, cols), F32),
            pltpu.VMEM((size, size), F32), pltpu.SemaphoreType.DMA((4,)),
        ],
        4, (), 62,
    )
    onehot = [pltpu.VMEM((n, n), BF16)]
    a_s, basis = call(
        k_sort, (order, local_inverse[0, 0], primal_basis[0, 0]), [b16(n, n), b16(n, modes)], 4 * n * n * n, onehot,
    )
    s_s, = call(k_sort, (order, schur[0, 0]), [b16(n, n)], 4 * n * n * n, onehot)
    got = exchange(*out, first=True, beside=(a_s,))
    first_b = got[1]

    res, product, direction = src, src, src
    directions = []
    sigma = centre / spread
    rho = 1.0 / sigma
    for step in range(ITERS):
        res, scaled, give, kept = call(
            partial(k_residual, step == 0, peers, size),
            (table, blocks, basis, res, product, *got),
            [full, b16(n, cols), f32(size, cols), f32(2 * size, cols)],
            2 * n * modes * cols, buf, after=(s_s,) if step == 0 else (),
        )
        from_a = pair(give, "A")
        mine, = call(partial(k_middle, size), (kept, from_a), [f32(2 * size, cols)], 0)
        theirs = pair(mine, "B")
        sol, sol_b = call(
            partial(k_coarse, size), (inv, first_b, mine, theirs), [f32(size, cols), f32(size, cols)],
            4 * size * size * cols,
        )
        sol_a = pair(sol, "A")
        up, *out = call(
            partial(k_update, peers, size),
            (table, blocks, basis, a_s, scaled, sol, sol_a, sol_b),
            [full] + sent, big, buf,
        )
        got = exchange(*out)
        if step == 0:
            keep, gain = None, 1.0 / centre
        else:
            rho_new = 1.0 / (2.0 * sigma - rho)
            keep, gain = rho_new * rho, 2.0 * rho_new / spread
            rho = rho_new
        direction, product, *out = call(
            partial(k_apply, keep, gain),
            (table, s_s, up, direction, *got),
            [full, full] + sent, big, buf,
        )
        directions.append(direction)
        beside = ()
        if step == ITERS - 1:
            total, token = call(k_solution, (order, *directions), [full, f32(8, 128)], 2 * big)
            beside = (token,)
        got = exchange(*out, beside=beside)
    residual, = call(k_final, (table, order, res, product, *got), [full], 2 * big, buf)
    return total[None, None], residual[None, None]


def solution(mesh):
    four = P("sx", "sy", None, None)
    three = P("sx", "sy", None)
    return jax.shard_map(
        body,
        mesh=mesh,
        in_specs=(four, four, four, four, four, three, three, three),
        out_specs=(four, four),
        check_vma=False,
    )
```

```python
from functools import partial

import jax
import jax.numpy as jnp
from jax import lax
from jax.experimental import pallas as pl
from jax.experimental.pallas import tpu as pltpu
from jax.sharding import PartitionSpec as P

MROW = 64
TILE = 8
ITERS = 3
centre = 1.6
spread = 1.4

SIDES = ((1, 1), (1, 0), (1, -1), (-1, 1), (-1, 0), (-1, -1), (0, 1), (0, -1))

VMEM = pl.BlockSpec(memory_space=pltpu.VMEM)
FAR = pl.BlockSpec(memory_space=pltpu.HBM)
LOOSE = pl.BlockSpec(memory_space=pl.ANY)
F32 = jnp.float32
BF16 = jnp.bfloat16
HIGH = lax.Precision.HIGHEST


def other(i, j, side):
    if side in "AB":
        return (i ^ 1 if side == "A" else ((i + 1) ^ 1) - 1), j
    return i, (j ^ 1 if (side == "C") == (i % 2 == 0) else ((j + 1) ^ 1) - 1)


def links(side):
    sizes = lax.axis_size("sx"), lax.axis_size("sy")
    for i in range(sizes[0]):
        for j in range(sizes[1]):
            yield sizes, (i, j), other(i, j, side)


def swap(x, side, wrap=False):
    pairs = []
    for (n, m), (i, j), (p, q) in links(side):
        if wrap or (0 <= p < n and 0 <= q < m):
            pairs.append((i * m + j, p % n * m + q % m))
    return lax.ppermute(x, ("sx", "sy"), pairs)


def leads(i, j, side):
    if side == "A":
        return 1 - i % 2
    if side == "B":
        return i % 2
    return (1 + i + j) % 2 if side == "C" else (i + j) % 2


def pair(x, side):
    pairs = []
    for (n, m), (i, j), (p, q) in links(side):
        if leads(i, j, side):
            pairs.append([i * m + j, p % n * m + q % m])
    return lax.all_gather(x, ("sx", "sy"), axis_index_groups=pairs, tiled=True)


def half_of(ref, side, rows, at=0, take=None):
    take = rows if take is None else take
    if ref.shape[0] != 2 * rows:
        return ref[at:at + take, :]
    return ref[pl.ds(pl.multiple_of(lax.rem(leads(*here(), side), 2) * rows, TILE) + at, take), :]


def here():
    return lax.axis_index("sx"), lax.axis_index("sy")


def table_of(counts):
    i, j = here()
    alpha = 1 - 2 * lax.rem(i, 2)
    gamma = 1 - 2 * lax.rem(i + j, 2)
    size = [counts[d] for d in range(8)]
    first = [jnp.int32(0)]
    for d in range(8):
        first.append(first[d] + size[d])
    starts, sizes = [], []
    for s, t in SIDES:
        raw = 3 * (s * alpha + 1) + (t * gamma + 1)
        d = jnp.where(raw > 4, raw - 1, raw)
        start, count = first[0], size[0]
        for e in range(1, 8):
            start = jnp.where(d == e, first[e], start)
            count = jnp.where(d == e, size[e], count)
        starts.append(start)
        sizes.append(count)
    return starts, sizes, first[8]


def groups_of(table):
    return [(table[0, k], table[0, 8 + k]) for k in range(8)]


def to_sorted(order, rows=None):
    n = order.shape[1]
    rows = n if rows is None else rows
    column = jnp.transpose(jnp.broadcast_to(order, (128, n)))[:rows, :1]
    return (lax.broadcasted_iota(jnp.int32, (rows, n), 1) == column).astype(F32).astype(BF16)


def from_sorted(order):
    n = order.shape[1]
    return (lax.broadcasted_iota(jnp.int32, (n, n), 0) == order).astype(F32).astype(BF16)


def moved(onehot, x):
    high = x.astype(BF16)
    rest = x - high.astype(F32)
    mid = rest.astype(BF16)
    low = (rest - mid.astype(F32)).astype(BF16)
    dot = partial(jnp.dot, onehot, preferred_element_type=F32)
    return dot(high) + dot(mid) + dot(low)


def window(start):
    skip = lax.rem(start, TILE)
    return pl.ds(pl.multiple_of(start - skip, TILE), MROW + TILE), skip


def emit(buf, groups, a_ref, b_ref, c_ref, d_ref):
    for k, (start, _) in enumerate(groups):
        place, skip = window(start)
        rows = pltpu.roll(buf[place, :], lax.rem(MROW + TILE - skip, MROW + TILE), 0)[0:MROW, :]
        if k < 3:
            a_ref[k * MROW:(k + 1) * MROW, :] = rows
        elif k < 6:
            b_ref[(k - 3) * MROW:(k - 2) * MROW, :] = rows
        elif k == 6:
            c_ref[...] = rows
        else:
            d_ref[...] = rows


def absorb(buf, groups, factor, ra, rb, rc, rd):
    edge_a = half_of(ra, "A", 3 * MROW, MROW, MROW)
    pieces = [half_of(rc, "C", 3 * MROW, k * MROW, MROW) for k in range(3)]
    order = (pieces[0], edge_a, rd[0:64, :], pieces[2], rb[64:128, :], rd[128:192, :], pieces[1], rd[64:128, :])
    at = lax.broadcasted_iota(jnp.int32, (MROW, 1), 0)
    tail = jnp.zeros((TILE, buf.shape[1]), F32)
    for (start, count), piece in zip(groups, order):
        place, skip = window(start)
        piece = jnp.concatenate([jnp.where(at < count, factor * piece, 0.0), tail], axis=0)
        buf[place, :] = buf[place, :] + pltpu.roll(piece, skip, 0)


def weights(n, table):
    total = jnp.max(table[1:2, :], axis=1, keepdims=True)
    return jnp.where(lax.broadcasted_iota(jnp.int32, (n, 1), 0) < total, 0.5, 1.0).astype(F32)


def chooser(blocks, peers, size):
    mine = lax.axis_index("sx")
    alpha = 1 - 2 * lax.rem(mine, 2)
    n = blocks.shape[1]
    rows = lax.broadcasted_iota(jnp.int32, (size, n), 0)
    parts = []
    for shift in (0, 1, -1):
        want = lax.rem(mine + shift * alpha + peers, peers) * size
        parts.append((blocks - want == rows).astype(F32))
    return jnp.concatenate(parts, axis=0)


def k_first(counts_in, order_in, source_in, table_ref, a_ref, b_ref, c_ref, d_ref,
            top, counts, order, source, arrived):
    copies = [
        pltpu.make_async_copy(src, dst, arrived.at[k])
        for k, (src, dst) in enumerate(((order_in, order), (counts_in, counts), (source_in, source)))
    ]
    for copy in copies:
        copy.start()
    copies[0].wait()
    onehot = to_sorted(order[...], top.shape[0])
    copies[1].wait()
    starts, sizes, total = table_of(counts)
    at = lax.broadcasted_iota(jnp.int32, table_ref.shape, 1)
    row = lax.broadcasted_iota(jnp.int32, table_ref.shape, 0)
    table = jnp.full(table_ref.shape, total, jnp.int32)
    for k, value in enumerate(starts + sizes):
        table = jnp.where((row == 0) & (at == k), value, table)
    table_ref[...] = table
    copies[2].wait()
    top[...] = moved(onehot, source[...])
    emit(top, list(zip(starts, sizes)), a_ref, b_ref, c_ref, d_ref)


def k_source(order, source, out):
    out[...] = moved(to_sorted(order[...]), source[...])


def k_relay(ra, rb, c, d, *rest):
    to_c, to_d = rest[-2:]
    to_c[0:64, :] = half_of(ra, "A", 3 * MROW, 2 * MROW, MROW)
    to_d[0:64, :] = half_of(ra, "A", 3 * MROW, 0, MROW)
    to_c[64:128, :] = c[...]
    to_d[64:128, :] = d[...]
    to_c[128:192, :] = rb[128:192, :]
    to_d[128:192, :] = rb[0:64, :]


def k_sort(order, matrix, *rest):
    onehot = rest[-1]
    onehot[...] = to_sorted(order[...])
    n = matrix.shape[0]
    step = 256
    dot = partial(lax.dot_general, preferred_element_type=F32)
    if len(rest) == 4:
        basis, out, basis_ref = rest[:3]
        basis_ref[...] = dot(onehot[...], basis[...], (((1,), (0,)), ((), ()))).astype(BF16)
    else:
        out = rest[0]
    for at in range(0, n, step):
        half = dot(onehot[at:at + step, :], matrix[...], (((1,), (0,)), ((), ()))).astype(BF16)
        out[at:at + step, :] = dot(half, onehot[...], (((1,), (1,)), ((), ()))).astype(BF16)


def k_residual(first, peers, size, table, blocks, basis, old, product, ra, rb, rc, rd,
               *rest):
    res_ref, scaled_ref, give_ref, keep_ref = rest[-4:]
    res_ref[...] = old[...] if first else old[...] - product[...]
    absorb(res_ref, groups_of(table), 1.0 if first else -1.0, ra, rb, rc, rd)
    n = old.shape[0]
    res = res_ref[...]
    scaled = (weights(n, table) * res).astype(BF16)
    scaled_ref[...] = scaled
    primal = lax.dot_general(basis[...], scaled, (((0,), (0,)), ((), ())), preferred_element_type=F32)
    select = chooser(blocks[...], peers, size)
    spread_out = jnp.dot(select, primal, precision=HIGH, preferred_element_type=F32)
    give_ref[...] = spread_out[size:2 * size, :]
    keep_ref[0:size, :] = spread_out[0:size, :]
    keep_ref[size:2 * size, :] = spread_out[2 * size:3 * size, :]


def k_middle(size, kept, from_a, *rest):
    mine = rest[-1]
    mine[0:size, :] = kept[0:size, :] + half_of(from_a, "A", size)
    mine[size:2 * size, :] = kept[size:2 * size, :]
    if len(rest) == 2:
        mine[2 * size:3 * size, :] = jnp.zeros((size, mine.shape[1]), F32)
        mine[2 * size:3 * size, 0:size] = rest[0][...]


def k_coarse(size, inv, first, mine, theirs, own_ref, b_ref):
    dot = partial(jnp.dot, precision=HIGH, preferred_element_type=F32)
    rows = mine.shape[0]
    their_own = half_of(theirs, "B", rows, 0, size)
    their_mine = half_of(theirs, "B", rows, size, size)
    inv_b = half_of(first, "B", 3 * size, 2 * size, size)[:, 0:size]
    own_ref[...] = dot(inv[...], mine[0:size, :] + their_mine)
    b_ref[...] = dot(inv_b, their_own + mine[size:2 * size, :])


def k_update(peers, size, table, blocks, basis, matrix, scaled, sol, sol_a, sol_b,
             up_ref, a_ref, b_ref, c_ref, d_ref):
    groups = groups_of(table)
    select = chooser(blocks[...], peers, size)
    stack = jnp.concatenate([sol[...], half_of(sol_a, "A", size), sol_b[...]], axis=0)
    picked = lax.dot_general(select, stack, (((0,), (0,)), ((), ())), precision=HIGH, preferred_element_type=F32)
    n = scaled.shape[0]
    up = jnp.dot(matrix[...], scaled[...], preferred_element_type=F32)
    up = up + jnp.dot(basis[...], picked.astype(BF16), preferred_element_type=F32)
    up = weights(n, table) * up
    up_ref[...] = up
    emit(up_ref, groups, a_ref, b_ref, c_ref, d_ref)


def k_apply(keep, gain, table, schur, up, old, ra, rb, rc, rd, dir_ref, v_ref, a_ref, b_ref, c_ref, d_ref):
    groups = groups_of(table)
    own = gain * up[...]
    dir_ref[...] = own if keep is None else keep * old[...] + own
    absorb(dir_ref, groups, gain, ra, rb, rc, rd)
    v_ref[...] = jnp.dot(schur[...], dir_ref[...].astype(BF16), preferred_element_type=F32)
    emit(v_ref, groups, a_ref, b_ref, c_ref, d_ref)


def k_solution(order, one, two, three, out, back):
    back[...] = from_sorted(order[...])
    out[...] = moved(back[...], one[...] + two[...] + three[...])


def k_final(table, back, old, product, ra, rb, rc, rd, out, buf):
    buf[...] = old[...] - product[...]
    absorb(buf, groups_of(table), -1.0, ra, rb, rc, rd)
    out[...] = moved(back[...], buf[...])


def call(kernel, ins, outs, flops, scratch=(), far=0, after=(), room=28):
    moved_bytes = sum(x.size * x.dtype.itemsize for x in ins)
    moved_bytes += sum(x.size * x.dtype.itemsize for x in outs)
    return pl.pallas_call(
        kernel,
        out_shape=tuple(outs),
        in_specs=[FAR] * far + [VMEM] * (len(ins) - far) + [LOOSE] * len(after),
        out_specs=tuple([VMEM] * len(outs)),
        scratch_shapes=list(scratch),
        compiler_params=pltpu.CompilerParams(vmem_limit_bytes=room * 1024 * 1024),
        cost_estimate=pl.CostEstimate(flops=flops, bytes_accessed=moved_bytes, transcendentals=0),
    )(*ins, *after)


def exchange(a, b, c, d, first=False, beside=()):
    leg = jax.ShapeDtypeStruct((3 * MROW, c.shape[1]), F32)
    rb = swap(b, "B")
    ra = pair(a, "A")
    to_c, to_d = call(k_relay, (ra, rb, c, d), [leg, leg], 0, after=beside)
    rd = swap(to_d, "D")
    rc = swap(to_c, "C") if first else pair(to_c, "C")
    return ra, rb, rc, rd


def body(local_source, schur, local_inverse, primal_basis, coarse_inverse, primal_map, shared_count, row_order):
    source = local_source[0, 0]
    n, cols = source.shape
    inv = coarse_inverse[0, 0]
    size = inv.shape[0]
    modes = primal_basis.shape[3]
    peers = lax.axis_size("sx")
    counts = shared_count[0, 0]
    order = row_order[0]
    blocks = primal_map[0]

    f32 = lambda *shape: jax.ShapeDtypeStruct(shape, F32)
    b16 = lambda *shape: jax.ShapeDtypeStruct(shape, BF16)
    full = f32(n, cols)
    sent = [f32(3 * MROW, cols), f32(3 * MROW, cols), f32(MROW, cols), f32(MROW, cols)]
    big = 2 * n * n * cols

    shared = 9 * MROW
    table, *out = call(
        k_first,
        (counts, order, source),
        [jax.ShapeDtypeStruct((8, 128), jnp.int32)] + sent,
        2 * big,
        [
            pltpu.VMEM((shared, cols), F32), pltpu.SMEM((8,), jnp.int32), pltpu.VMEM(order.shape, jnp.int32),
            pltpu.VMEM((n, cols), F32), pltpu.SemaphoreType.DMA((3,)),
        ],
        3, (), 62,
    )
    src, = call(k_source, (order, source), [full], 3 * big)
    onehot = [pltpu.VMEM((n, n), BF16)]
    a_s, basis = call(
        k_sort, (order, local_inverse[0, 0], primal_basis[0, 0]), [b16(n, n), b16(n, modes)], 4 * n * n * n, onehot,
    )
    s_s, = call(k_sort, (order, schur[0, 0]), [b16(n, n)], 4 * n * n * n, onehot)
    got = exchange(*out, first=True, beside=(a_s,))

    res, product, direction = src, src, src
    directions = []
    sigma = centre / spread
    rho = 1.0 / sigma
    for step in range(ITERS):
        res, scaled, give, kept = call(
            partial(k_residual, step == 0, peers, size),
            (table, blocks, basis, res, product, *got),
            [full, b16(n, cols), f32(size, cols), f32(2 * size, cols)],
            2 * n * modes * cols, after=(s_s,) if step == 0 else (),
        )
        from_a = pair(give, "A")
        extra = (inv,) if step == 0 else ()
        mine, = call(partial(k_middle, size), (kept, from_a) + extra, [f32((2 + len(extra)) * size, cols)], 0)
        theirs = pair(mine, "B")
        first = theirs if step == 0 else first
        sol, sol_b = call(
            partial(k_coarse, size), (inv, first, mine, theirs), [f32(size, cols), f32(size, cols)],
            4 * size * size * cols,
        )
        sol_a = pair(sol, "A")
        up, *out = call(
            partial(k_update, peers, size),
            (table, blocks, basis, a_s, scaled, sol, sol_a, sol_b),
            [full] + sent, big,
        )
        got = exchange(*out)
        if step == 0:
            keep, gain = None, 1.0 / centre
        else:
            rho_new = 1.0 / (2.0 * sigma - rho)
            keep, gain = rho_new * rho, 2.0 * rho_new / spread
            rho = rho_new
        direction, product, *out = call(
            partial(k_apply, keep, gain),
            (table, s_s, up, direction, *got),
            [full, full] + sent, big,
        )
        directions.append(direction)
        beside = ()
        if step == ITERS - 1:
            total, back = call(k_solution, (order, *directions), [full, b16(n, n)], 3 * big)
            beside = (back,)
        got = exchange(*out, beside=beside)
    residual, = call(k_final, (table, back, res, product, *got), [full], 3 * big, [pltpu.VMEM((n, cols), F32)])
    return total[None, None], residual[None, None]


def solution(mesh):
    four = P("sx", "sy", None, None)
    three = P("sx", "sy", None)
    return jax.shard_map(
        body,
        mesh=mesh,
        in_specs=(four, four, four, four, four, three, three, three),
        out_specs=(four, four),
        check_vma=False,
    )
```
